32 devices in a mesh: groups: 2 (over x), atoms: 16 (over z, y, core).
Axes of the slice: x: 2, y: 2, z: 4, core: 2. Of those that a mesh axis runs over, the one named last changes fastest.
Arguments:
- node_feat: bfloat16 [2048, 128], P(('groups', 'atoms')), parts along dimension 0, may hold values from -6 to 6
- species: int32 [2048], P(('groups', 'atoms')), parts along dimension 0, may hold values from 0 to 1
- positions: float32 [2048, 3], P(('groups', 'atoms')), parts along dimension 0, may hold values from 0 to 12
- pair_second: int32 [65536], P(('groups', 'atoms')), parts along dimension 0, may hold values from 0 to 127
- pair_mask: int32 [65536], P(('groups', 'atoms')), parts along dimension 0, may hold values 0 or 1
- x_vec: bfloat16 [26624, 512], P(('groups', 'atoms')), parts along dimension 0, may hold values from -6 to 6
- species_table: bfloat16 [2, 128], replicated, may hold values from -4 to 4
- onsite_table: float32 [2, 13], replicated, may hold values from -1 to 1
- w_first: bfloat16 [128, 256], replicated, may hold values from -0.375 to 0.375
- w_second: bfloat16 [128, 256], replicated, may hold values from -0.375 to 0.375
- w_radial: bfloat16 [32, 256], replicated, may hold values from -1 to 1
- w_out: bfloat16 [256, 169], replicated, may hold values from -0.375 to 0.375
Outputs:
- first_step: bfloat16 [26624, 512], P(('groups', 'atoms')), parts along dimension 0
- filtered: float32 [26624, 512], P(('groups', 'atoms')), parts along dimension 0
The draws below stay inside these ranges and needn't reach their ends.
There are 2 independent parts, one for each index of `groups`. The reference program is written for one: setup_inputs(seed, part) draws one part's arguments, and reference() takes and returns one part's arrays. A program takes and returns all parts, laid end to end along the dimension named above; an argument that names none is the same for every part. Nothing has to cross between parts.
All inputs are finite; a program needn't handle non-finite values. No bound on the sum of `pair_mask` on one device may be relied on, other than what follows from the above.
Results may differ from the reference program's by a relative error of at most 0.0058.
Values may be sent and summed in bfloat16 or wider, within the bound.
A program may use at most 128 MiB of HBM per device.

```python
import jax
import jax.numpy as jnp
from jax import lax

ORB = 13
F = 128
HID = 256
NRBF = 32
SPECIES = 2
COLS = 512
NEIGH = 32
ATOM_DEV = 64
PAIRS_DEV = 2048
ATOMS = 1024
PAIRS = 32768
ORBS = 13312
N_ATOMS = 16


def touch_ends(values, own_key, low, high):
    longest = values.shape.index(max(values.shape))
    spots = []
    for shift in (0, 1):
        where = [jax.random.randint(jax.random.fold_in(own_key, axis), (), 0, length) for axis, length in enumerate(values.shape)]
        where[longest] = (where[longest] + shift) % values.shape[longest]
        spots.append(tuple(where))
    return values.at[spots[0]].set(low).at[spots[1]].set(high)


def block_levels(own_key, extent, pieces, smallest, top_value):
    loudness, own = 1.0, jax.random.fold_in(own_key, 6)
    for axis_at, blocks in pieces:
        heights = jnp.exp(jax.random.uniform(jax.random.fold_in(own, axis_at), (blocks,), jnp.float32, smallest / len(pieces), top_value / len(pieces)))
        loudness = loudness * jnp.repeat(heights, extent[axis_at] // blocks).reshape([-1 if axis == axis_at else 1 for axis in range(len(extent))])
    return loudness


def bell_draw(own_key, dims, spread, most, split=(), kind=jnp.bfloat16):
    entries = spread * jax.random.normal(own_key, dims, jnp.float32)
    if split:
        entries = entries * block_levels(own_key, dims, split, -0.22, 0.18)
    return jnp.clip(entries, -most, most).astype(kind)


def setup_inputs(seed: int = 0, part: int = 0) -> dict:
    key_list = jax.random.split(jax.random.key(seed), 13)
    part_keys = jax.random.split(jax.random.fold_in(key_list[12], part), 13)
    node_feat = bell_draw(part_keys[0], (ATOMS, F), 1.0, 6.0, ((0, 16),))
    species = touch_ends(jax.random.randint(part_keys[1], (ATOMS,), 0, SPECIES), jax.random.fold_in(part_keys[1], 1), 0, SPECIES - 1).astype(jnp.int32)
    positions = jnp.clip(12.0 * jax.random.uniform(part_keys[2], (ATOMS, 3), jnp.float32) ** block_levels(part_keys[2], (ATOMS, 3), ((0, 16),), -0.2, 0.2), 0.0, 12.0)
    pair_second = touch_ends(jax.random.randint(part_keys[3], (PAIRS,), 0, 2 * ATOM_DEV), jax.random.fold_in(part_keys[3], 1), 0, (2 * ATOM_DEV) - 1).astype(jnp.int32)
    pair_mask = touch_ends((jax.random.randint(part_keys[4], (PAIRS,), 0, 4) < 3).astype(jnp.int32), jax.random.fold_in(part_keys[4], 1), 0, 1)
    x_vec = bell_draw(part_keys[5], (ORBS, COLS), 1.0, 6.0, ((0, 16),))
    species_table = bell_draw(key_list[6], (SPECIES, F), 1.0, 4.0)
    onsite_table = jnp.clip(jax.random.uniform(key_list[7], (SPECIES, ORB), jnp.float32, -1.0, 1.0), -1.0, 1.0)
    w_first = bell_draw(key_list[8], (F, HID), (2 * F) ** -0.5, 0.375)
    w_second = bell_draw(key_list[9], (F, HID), (2 * F) ** -0.5, 0.375)
    w_radial = bell_draw(key_list[10], (NRBF, HID), NRBF ** -0.5, 1.0)
    w_out = bell_draw(key_list[11], (HID, ORB * ORB), HID ** -0.5, 0.375)
    return dict(node_feat=node_feat, species=species, positions=positions, pair_second=pair_second, pair_mask=pair_mask, x_vec=x_vec, species_table=species_table, onsite_table=onsite_table, w_first=w_first, w_second=w_second, w_radial=w_radial, w_out=w_out)


def block_matrices(feat, next_feat, pos, next_pos, second, mask, w_first, w_second, w_radial, w_out):
    count = feat.shape[0]
    first = jnp.repeat(jnp.arange(count, dtype=jnp.int32), NEIGH)
    window_feat = jnp.concatenate([feat, next_feat], axis=0)
    window_pos = jnp.concatenate([pos, next_pos], axis=0)
    diff = pos[first] - window_pos[second]
    dist_sq = lax.optimization_barrier(jnp.sum(diff * diff, axis=-1))
    centres = jnp.arange(NRBF, dtype=jnp.float32) * (2.0 / (NRBF - 1))
    radial = jnp.exp(-((dist_sq[:, None] / 64.0 - centres[None, :]) * 8.0) ** 2).astype(jnp.bfloat16)
    pre = jnp.dot(feat[first], w_first, preferred_element_type=jnp.float32)
    pre = pre + jnp.dot(window_feat[second], w_second, preferred_element_type=jnp.float32)
    pre = pre + jnp.dot(radial, w_radial, preferred_element_type=jnp.float32)
    hidden = jax.nn.silu(pre).astype(jnp.bfloat16)
    factor = mask.astype(jnp.float32) / jnp.sqrt(jnp.float32(2 * ORB * NEIGH))
    blocks = jnp.dot(hidden, w_out, preferred_element_type=jnp.float32) * factor[:, None]
    slot_index = first * (2 * count) + second
    summed = jax.ops.segment_sum(blocks, slot_index, num_segments=2 * count * count)
    summed = summed.reshape(count, 2 * count, ORB, ORB)
    own = summed[:, :count]
    upper = summed[:, count:]
    square = own + own.transpose(1, 0, 3, 2)
    square = square.transpose(0, 2, 1, 3).reshape(count * ORB, count * ORB).astype(jnp.bfloat16)
    upper = upper.transpose(0, 2, 1, 3).reshape(count * ORB, count * ORB).astype(jnp.bfloat16)
    return (square, upper)

def reference(node_feat, species, positions, pair_second, pair_mask, x_vec, species_table, onsite_table, w_first, w_second, w_radial, w_out):
    blocks_n = N_ATOMS
    count = ATOM_DEV
    onehot = (species[:, None] == jnp.arange(SPECIES, dtype=jnp.int32)[None, :]).astype(jnp.bfloat16)
    feat = (node_feat.astype(jnp.float32) + jnp.dot(onehot, species_table, preferred_element_type=jnp.float32)).astype(jnp.bfloat16)
    onsite = jnp.dot(onehot.astype(jnp.float32), onsite_table, precision=lax.Precision.HIGHEST).reshape(ATOMS * ORB)
    feat_b = feat.reshape(blocks_n, count, F)
    pos_b = positions.reshape(blocks_n, count, 3)
    second_b = pair_second.reshape(blocks_n, PAIRS_DEV)
    mask_b = pair_mask.reshape(blocks_n, PAIRS_DEV)

    def one_block(items):
        return block_matrices(items[0], items[1], items[2], items[3], items[4], items[5], w_first, w_second, w_radial, w_out)
    square_all, upper_all = lax.map(one_block, (feat_b, jnp.roll(feat_b, -1, 0), pos_b, jnp.roll(pos_b, -1, 0), second_b, mask_b))
    upper_prev = jnp.roll(upper_all, 1, 0)

    def apply(vec):
        vec_b = vec.reshape(blocks_n, count * ORB, COLS)

        def one_apply(items):
            square, upper, lower, here, after, before = items
            result = jnp.dot(square, here, preferred_element_type=jnp.float32)
            result = result + jnp.dot(upper, after, preferred_element_type=jnp.float32)
            return result + jnp.dot(lower.T, before, preferred_element_type=jnp.float32)
        result = lax.map(one_apply, (square_all, upper_all, upper_prev, vec_b, jnp.roll(vec_b, -1, 0), jnp.roll(vec_b, 1, 0)))
        result = result.reshape(ATOMS * ORB, COLS)
        return result + onsite[:, None] * vec.astype(jnp.float32)
    first_step = apply(x_vec).astype(jnp.bfloat16)
    filtered = 2.0 * apply(first_step) - x_vec.astype(jnp.float32)
    return (first_step, filtered)
```

```python
import functools

import jax
import jax.numpy as jnp
from jax import lax
from jax.experimental import pallas as pl
from jax.experimental.pallas import tpu as pltpu
from jax.sharding import PartitionSpec as P

ORB = 13
NRBF = 32
SPECIES = 2
NEIGH = 32
MESH = pl.DeviceIdType.MESH
F32, BF16 = jnp.float32, jnp.bfloat16
CHUNK = 512
GROUP = 8
COLS_STEP = 256


def dot(a, b):
    return jnp.dot(a, b, preferred_element_type=F32)


def dot_tn(a, b):
    return lax.dot_general(a, b, (((0,), (0,)), ((), ())), preferred_element_type=F32)


def dot_nt(a, b):
    return lax.dot_general(a, b, (((1,), (1,)), ((), ())), preferred_element_type=F32)


def split_two(v):
    high = v.astype(BF16)
    return [high, (v - high.astype(F32)).astype(BF16)]


def split_three(v):
    high = v.astype(BF16).astype(F32)
    rest = v - high
    middle = rest.astype(BF16).astype(F32)
    return jnp.concatenate([high, middle, rest - middle, jnp.zeros_like(v)], 0).astype(BF16)


def pair_tiles(own_code_at, pos_first, pos_window, terms, w_out, scale, width, tiles):
    count = tiles.shape[1]
    per_chunk = CHUNK // NEIGH
    lanes = lax.broadcasted_iota(jnp.int32, (1, CHUNK), 1) // NEIGH
    atom = lax.broadcasted_iota(jnp.int32, (count, CHUNK), 0)
    second = lax.broadcasted_iota(jnp.int32, (128, CHUNK), 0)
    centres = lax.broadcasted_iota(jnp.int32, (NRBF, 1), 0).astype(F32) * (2.0 / (NRBF - 1))
    diagonal = (
        lax.broadcasted_iota(jnp.int32, (GROUP, GROUP * NEIGH), 1) // NEIGH
        == lax.broadcasted_iota(jnp.int32, (GROUP, GROUP * NEIGH), 0)
    ).astype(F32)
    pairs = tiles.shape[0]

    @pl.loop(0, count // per_chunk)
    def _(at):
        code = own_code_at(at)
        pick_first = (atom == lanes + at * per_chunk).astype(F32).astype(BF16)
        pick_all = (second == code).astype(F32).astype(BF16)
        pick_second = pick_all[:width]
        parts = dot(pos_first, pick_first) - dot(pos_window, pick_second)
        diff = parts[0:8] + parts[8:16] + parts[16:24]
        dist_sq = jnp.sum(diff * diff, axis=0, keepdims=True)
        radial = jnp.exp(-(((dist_sq / 64.0 - centres) * 8.0) ** 2)).astype(BF16)
        picks = jnp.concatenate([pick_first, pick_first, pick_second, pick_second, radial], 0)
        pre = dot(terms, picks)
        half = pre * 0.5
        hidden = (half + half * jnp.tanh(half)).astype(BF16)
        blocks = dot(w_out, hidden) * scale
        for group in range(per_chunk // GROUP):
            span = slice(group * GROUP * NEIGH, (group + 1) * GROUP * NEIGH)
            spread = (blocks[:, None, span] * diagonal[None]).reshape(pairs * GROUP, GROUP * NEIGH)
            placed = dot_nt(spread.astype(BF16), pick_all[:, span])
            start = pl.multiple_of((at * (per_chunk // GROUP) + group) * GROUP, GROUP)
            tiles[:, pl.ds(start, GROUP), :] = placed.reshape(pairs, GROUP, 128)


def kernel(
    node_feat,
    species,
    positions,
    pair_second,
    pair_mask,
    x_vec,
    species_table,
    onsite_table,
    w_first,
    w_second,
    w_radial,
    w_out,
    first_out,
    filtered_out,
    feats,
    poss,
    codes,
    rows,
    xx,
    yy,
    tiles_own,
    tiles_prev,
    right_mat,
    left_mat,
    small_send,
    small_recv,
    x_send,
    x_recv,
    y_send,
    y_recv,
):
    n = lax.axis_size("atoms")
    me = lax.axis_index("atoms")
    right, left = lax.rem(me + 1, n), lax.rem(me + n - 1, n)
    count = node_feat.shape[0]
    cols = x_vec.shape[1]
    lane_blocks = cols // 128

    barrier = pltpu.get_barrier_semaphore()
    for neighbour in (left, right):
        pl.semaphore_signal(barrier, inc=1, device_id={"atoms": neighbour}, device_id_type=MESH)

    def send(src, dst, send_sem, recv_sem, to):
        copy = pltpu.make_async_remote_copy(
            src_ref=src,
            dst_ref=dst,
            send_sem=send_sem,
            recv_sem=recv_sem,
            device_id={"atoms": to},
            device_id_type=MESH,
        )
        copy.start()
        return copy

    spec = species[...]
    onehot = (lax.broadcasted_iota(jnp.int32, (SPECIES, count), 0) == spec).astype(F32)
    feat = (
        node_feat[...].astype(F32) + dot_tn(onehot.astype(BF16), species_table[...])
    ).astype(BF16)
    feats[1] = feat
    poss[1] = jnp.zeros(poss.shape[1:], F32)
    poss[1, 0:3, 0:count] = positions[...]
    codes[1] = jnp.where(pair_mask[...] != 0, pair_second[...], 255)
    pl.semaphore_wait(barrier, 2)

    small = [
        send(feats.at[1], feats.at[0], small_send.at[0], small_recv.at[0], right),
        send(feats.at[1], feats.at[2], small_send.at[1], small_recv.at[1], left),
        send(poss.at[1], poss.at[0], small_send.at[2], small_recv.at[2], right),
        send(poss.at[1], poss.at[2], small_send.at[3], small_recv.at[3], left),
        send(codes.at[1], codes.at[0], small_send.at[4], small_recv.at[4], right),
    ]

    for k in range(lane_blocks):
        rows[k] = x_vec[:, k * 128 : (k + 1) * 128].astype(F32)
    for k in range(lane_blocks):
        for i in range(ORB):
            xx[i, count : 2 * count, k * 128 : (k + 1) * 128] = rows[
                k, pl.ds(i, count, stride=ORB), :
            ].astype(BF16)
    x_copies = [
        send(
            xx.at[:, count : 2 * count, :],
            xx.at[:, 0:count, :],
            x_send.at[0],
            x_recv.at[0],
            right,
        ),
        send(
            xx.at[:, count : 2 * count, :],
            xx.at[:, 2 * count : 3 * count, :],
            x_send.at[1],
            x_recv.at[1],
            left,
        ),
    ]

    scale = 1.0 / jnp.sqrt(jnp.float32(2 * ORB * NEIGH))
    second_own = dot(feat, w_second[...])
    pos_own = split_three(poss[1][:, 0:count])
    onsite = lax.dot_general(
        onehot,
        onsite_table[...],
        (((0,), (0,)), ((), ())),
        precision=lax.Precision.HIGHEST,
        preferred_element_type=F32,
    )

    small[1].wait_recv()
    small[3].wait_recv()
    window = jnp.concatenate([second_own, dot(feats[2], w_second[...])], 0)
    terms = jnp.concatenate(
        split_two(dot(feat, w_first[...])) + split_two(window) + [w_radial[...]], 0
    )
    pos_window = jnp.concatenate([pos_own, split_three(poss[2][:, 0:count])], 1)

    def code_own(at):
        return codes[1, :, pl.ds(pl.multiple_of(at * CHUNK, CHUNK), CHUNK)]

    pair_tiles(
        code_own, pos_own, pos_window, terms.astype(F32).T.astype(BF16), w_out[...], scale,
        2 * count, tiles_own,
    )

    for k in (0, 2, 4):
        small[k].wait_recv()

    def code_prev(at):
        code = codes[0, :, pl.ds(pl.multiple_of(at * CHUNK, CHUNK), CHUNK)]
        return jnp.where(code < count, 255, code - count)

    terms = jnp.concatenate(
        split_two(dot(feats[0], w_first[...])) + split_two(second_own) + [w_radial[...]], 0
    )
    pair_tiles(
        code_prev, split_three(poss[0][:, 0:count]), pos_own,
        terms.astype(F32).T.astype(BF16), w_out[...], scale, count, tiles_prev,
    )

    @pl.loop(0, ORB)
    def _(i):
        for j in range(ORB):
            own = tiles_own[i * ORB + j]
            right_mat[pl.ds(pl.multiple_of(i * count, count), count), j * 128 : (j + 1) * 128] = (
                own.astype(BF16)
            )
            both = jnp.concatenate([tiles_prev[i * ORB + j], own], 0)
            left_mat[
                j * count : (j + 1) * count, pl.ds(pl.multiple_of(i * 128, 128), 128)
            ] = both.T[0:count].astype(BF16)

    def apply(vec, at):
        span = slice(at * COLS_STEP, (at + 1) * COLS_STEP)
        after = vec[:, count : 3 * count, span].reshape(ORB * 2 * count, COLS_STEP)
        before = vec[:, 0 : 2 * count, span].reshape(ORB * 2 * count, COLS_STEP)
        result = dot(right_mat[...], after) + dot(left_mat[...], before)
        here = vec[:, count : 2 * count, span].astype(F32)
        return [
            result[i * count : (i + 1) * count] + onsite[:, i : i + 1] * here[i]
            for i in range(ORB)
        ]

    for copy in x_copies:
        copy.wait_recv()
    y_copies = []
    for at in range(cols // COLS_STEP):
        span = slice(at * COLS_STEP, (at + 1) * COLS_STEP)
        step = apply(xx, at)
        for i in range(ORB):
            yy[i, count : 2 * count, span] = step[i].astype(BF16)
        for side, (place, to) in enumerate(((0, right), (2, left))):
            y_copies.append(
                send(
                    yy.at[:, count : 2 * count, span],
                    yy.at[:, place * count : (place + 1) * count, span],
                    y_send.at[2 * at + side],
                    y_recv.at[2 * at + side],
                    to,
                )
            )
        for i in range(ORB):
            for k in range(COLS_STEP // 128):
                rows[at * (COLS_STEP // 128) + k, pl.ds(i, count, stride=ORB), :] = step[i][
                    :, k * 128 : (k + 1) * 128
                ]
    for k in range(lane_blocks):
        first_out[:, k * 128 : (k + 1) * 128] = rows[k].astype(BF16)

    for at in range(cols // COLS_STEP):
        span = slice(at * COLS_STEP, (at + 1) * COLS_STEP)
        y_copies[2 * at].wait_recv()
        y_copies[2 * at + 1].wait_recv()
        step = apply(yy, at)
        for i in range(ORB):
            value = 2.0 * step[i] - xx[i, count : 2 * count, span].astype(F32)
            for k in range(COLS_STEP // 128):
                rows[at * (COLS_STEP // 128) + k, pl.ds(i, count, stride=ORB), :] = value[
                    :, k * 128 : (k + 1) * 128
                ]
        for k in range(COLS_STEP // 128):
            spot = at * (COLS_STEP // 128) + k
            filtered_out[:, spot * 128 : (spot + 1) * 128] = rows[spot]

    for copy in small + x_copies + y_copies:
        copy.wait_send()


def on_device(
    node_feat,
    species,
    positions,
    pair_second,
    pair_mask,
    x_vec,
    species_table,
    onsite_table,
    w_first,
    w_second,
    w_radial,
    w_out,
):
    count = node_feat.shape[0]
    orbs, cols = x_vec.shape
    slots = pair_second.shape[0]
    steps = cols // COLS_STEP
    vmem = pl.BlockSpec(memory_space=pltpu.VMEM)
    return pl.pallas_call(
        kernel,
        out_shape=(
            jax.ShapeDtypeStruct((orbs, cols), BF16),
            jax.ShapeDtypeStruct((orbs, cols), F32),
        ),
        in_specs=[vmem] * 12,
        out_specs=(vmem, vmem),
        scratch_shapes=[
            pltpu.VMEM((3, count, node_feat.shape[1]), BF16),
            pltpu.VMEM((3, 8, 128), F32),
            pltpu.VMEM((2, 1, slots), jnp.int32),
            pltpu.VMEM((cols // 128, orbs, 128), F32),
            pltpu.VMEM((ORB, 3 * count, cols), BF16),
            pltpu.VMEM((ORB, 3 * count, cols), BF16),
            pltpu.VMEM((ORB * ORB, count, 128), F32),
            pltpu.VMEM((ORB * ORB, count, 128), F32),
            pltpu.VMEM((orbs, ORB * 128), BF16),
            pltpu.VMEM((orbs, ORB * 128), BF16),
            pltpu.SemaphoreType.DMA((5,)),
            pltpu.SemaphoreType.DMA((5,)),
            pltpu.SemaphoreType.DMA((2,)),
            pltpu.SemaphoreType.DMA((2,)),
            pltpu.SemaphoreType.DMA((2 * steps,)),
            pltpu.SemaphoreType.DMA((2 * steps,)),
        ],
        compiler_params=pltpu.CompilerParams(
            collective_id=0, has_side_effects=True, vmem_limit_bytes=56 * 2**20
        ),
        name="pair_filter",
    )(
        node_feat,
        species.reshape(1, count),
        positions.T,
        pair_second.reshape(1, slots),
        pair_mask.reshape(1, slots),
        x_vec,
        species_table,
        onsite_table,
        w_first,
        w_second,
        w_radial,
        w_out.T,
    )


def solution(mesh):
    split = P(("groups", "atoms"))
    rows = P(("groups", "atoms"), None)
    return jax.shard_map(
        on_device,
        mesh=mesh,
        in_specs=(rows, split, rows, split, split, rows) + (P(),) * 6,
        out_specs=(rows, rows),
        check_vma=False,
    )
```

```python
import functools

import jax
import jax.numpy as jnp
from jax import lax
from jax.experimental import pallas as pl
from jax.experimental.pallas import tpu as pltpu
from jax.sharding import PartitionSpec as P

ORB = 13
NRBF = 32
SPECIES = 2
NEIGH = 32
MESH = pl.DeviceIdType.MESH
F32, BF16 = jnp.float32, jnp.bfloat16
CHUNK = 512
GROUP = 8
COLS_STEP = 256
SEND_STEP = 128


def dot(a, b):
    return jnp.dot(a, b, preferred_element_type=F32)


def dot_tn(a, b):
    return lax.dot_general(a, b, (((0,), (0,)), ((), ())), preferred_element_type=F32)


def dot_nt(a, b):
    return lax.dot_general(a, b, (((1,), (1,)), ((), ())), preferred_element_type=F32)


def split_two(v):
    high = v.astype(BF16)
    return [high, (v - high.astype(F32)).astype(BF16)]


def split_three(v):
    high = v.astype(BF16).astype(F32)
    rest = v - high
    middle = rest.astype(BF16).astype(F32)
    return jnp.concatenate([high, middle, rest - middle, jnp.zeros_like(v)], 0).astype(BF16)


def pair_tiles(own_code_at, pos_first, pos_window, terms, w_out, scale, width, tiles):
    count = tiles.shape[1]
    per_chunk = CHUNK // NEIGH
    lanes = lax.broadcasted_iota(jnp.int32, (1, CHUNK), 1) // NEIGH
    atom = lax.broadcasted_iota(jnp.int32, (count, CHUNK), 0)
    second = lax.broadcasted_iota(jnp.int32, (128, CHUNK), 0)
    centres = lax.broadcasted_iota(jnp.int32, (NRBF, 1), 0).astype(F32) * (2.0 / (NRBF - 1))
    diagonal = (
        lax.broadcasted_iota(jnp.int32, (GROUP, GROUP * NEIGH), 1) // NEIGH
        == lax.broadcasted_iota(jnp.int32, (GROUP, GROUP * NEIGH), 0)
    ).astype(F32)
    pairs = tiles.shape[0]

    @pl.loop(0, count // per_chunk)
    def _(at):
        code = own_code_at(at)
        pick_first = (atom == lanes + at * per_chunk).astype(F32).astype(BF16)
        pick_all = (second == code).astype(F32).astype(BF16)
        pick_second = pick_all[:width]
        parts = dot(pos_first, pick_first) - dot(pos_window, pick_second)
        diff = (parts[0:8] + parts[8:16] + parts[16:24])[0:3]
        dist_sq = jnp.sum(diff * diff, axis=0, keepdims=True)
        radial = jnp.exp(-(((dist_sq / 64.0 - centres) * 8.0) ** 2)).astype(BF16)
        picks = jnp.concatenate([pick_first, pick_first, pick_second, pick_second, radial], 0)
        pre = dot(terms, picks)
        half = pre * 0.5
        hidden = (half + half * jnp.tanh(half)).astype(BF16)
        blocks = dot(w_out, hidden) * scale
        for group in range(per_chunk // GROUP):
            span = slice(group * GROUP * NEIGH, (group + 1) * GROUP * NEIGH)
            spread = (blocks[:, None, span] * diagonal[None]).reshape(pairs * GROUP, GROUP * NEIGH)
            placed = dot_nt(spread.astype(BF16), pick_all[:, span])
            start = pl.multiple_of((at * (per_chunk // GROUP) + group) * GROUP, GROUP)
            tiles[:, pl.ds(start, GROUP), :] = placed.reshape(pairs, GROUP, 128)


def kernel(
    node_feat,
    species,
    positions,
    pair_second,
    pair_mask,
    x_vec,
    species_table,
    onsite_table,
    w_first,
    w_second,
    w_radial,
    w_out,
    first_out,
    filtered_out,
    feats,
    poss,
    codes,
    rows,
    xx,
    yy,
    tiles,
    right_mat,
    left_mat,
    small_send,
    small_recv,
    peer_send,
    cross_send,
    pass_send,
    x_recv,
    y_send,
    y_recv,
):
    n = lax.axis_size("atoms")
    me = lax.axis_index("atoms")
    spot = lax.rem(me, 4)
    odd = lax.rem(me, 2)
    own = 2 - odd
    peer = me + 1 - 2 * odd
    peer_place = 3 * odd
    upper_half = spot // 2
    cross_to = me - spot + 2 - upper_half
    middle = (spot == 1) | (spot == 2)
    pass_to = lax.rem(jnp.where(spot == 1, me + 3, me + n - 3), n)
    pass_from = 2 - 2 * upper_half
    pass_place = 2 * upper_half
    count = node_feat.shape[0]
    cols = x_vec.shape[1]
    lane_blocks = cols // 128
    pieces = cols // SEND_STEP

    def at_distance(d):
        return lax.rem(me + n + d, n)

    near = (-2, -1, 1, 2)
    barrier = pltpu.get_barrier_semaphore()
    for d in (-3, -2, -1, 1, 2, 3):
        pl.semaphore_signal(barrier, inc=1, device_id={"atoms": at_distance(d)}, device_id_type=MESH)

    def message(src, dst, send_sem, recv_sem, to):
        return pltpu.make_async_remote_copy(
            src_ref=src,
            dst_ref=dst,
            send_sem=send_sem,
            recv_sem=recv_sem,
            device_id={"atoms": to},
            device_id_type=MESH,
        )

    spec = species[...]
    onehot = (lax.broadcasted_iota(jnp.int32, (SPECIES, count), 0) == spec).astype(F32)
    feats[2] = (
        node_feat[...].astype(F32) + dot_tn(onehot.astype(BF16), species_table[...])
    ).astype(BF16)
    poss[2] = jnp.zeros(poss.shape[1:], F32)
    poss[2, 0:3, 0:count] = positions[...]
    poss[2, 3:4, 0:count] = spec.astype(F32)
    codes[2] = jnp.where(pair_mask[...] != 0, pair_second[...], 255)
    pl.semaphore_wait(barrier, 6)

    small = []
    for which, d in enumerate(near):
        for kind, array in enumerate((feats, poss, codes)):
            small.append(
                message(
                    array.at[2],
                    array.at[2 - d],
                    small_send.at[3 * which + kind],
                    small_recv.at[3 * which + kind],
                    at_distance(d),
                )
            )
    for copy in small:
        copy.start()

    def place(where):
        return pl.ds(pl.multiple_of(where * count, count), count)

    def x_message(from_place, to_place, piece, send_sem, to):
        span = slice(piece * SEND_STEP, (piece + 1) * SEND_STEP)
        return message(
            xx.at[:, place(from_place), span],
            xx.at[:, place(to_place), span],
            send_sem,
            x_recv.at[to_place, piece],
            to,
        )

    def cross_message(piece):
        return x_message(own, spot, piece, cross_send.at[piece], cross_to)

    def peer_message(piece):
        return x_message(own, peer_place, piece, peer_send.at[piece], peer)

    def pass_message(step, piece):
        return x_message(
            pass_from + step, pass_place + step, piece, pass_send.at[step, piece], pass_to
        )

    def arrived(where, piece):
        span = slice(piece * SEND_STEP, (piece + 1) * SEND_STEP)
        there = xx.at[:, place(where), span]
        message(there, there, peer_send.at[piece], x_recv.at[where, piece], peer).wait_recv()

    for k in range(lane_blocks):
        rows[k] = x_vec[:, k * 128 : (k + 1) * 128].astype(F32)
        for i in range(ORB):
            xx[i, place(own), k * 128 : (k + 1) * 128] = rows[
                k, pl.ds(i, count, stride=ORB), :
            ].astype(BF16)
        cross_message(k).start()
    for piece in range(pieces):
        peer_message(piece).start()

    scale = 1.0 / jnp.sqrt(jnp.float32(2 * ORB * NEIGH))
    base = 2 - own
    for copy in small:
        copy.wait_recv()

    seconds = [dot(feats[base + k], w_second[...]) for k in range(4)]
    sites = [split_three(poss[base + k][:, 0:count]) for k in range(4)]

    def network(k):
        window = jnp.concatenate([seconds[k], seconds[k + 1]], 0)
        terms = jnp.concatenate(
            split_two(dot(feats[base + k], w_first[...])) + split_two(window) + [w_radial[...]], 0
        )

        def code(at):
            return codes[base + k, :, pl.ds(pl.multiple_of(at * CHUNK, CHUNK), CHUNK)]

        pair_tiles(
            code, sites[k], jnp.concatenate([sites[k], sites[k + 1]], 1),
            terms.astype(F32).T.astype(BF16), w_out[...], scale, 2 * count, tiles.at[k],
        )

    def hand_on(piece):
        @pl.when(middle)
        def _():
            for step in range(2):
                arrived(pass_from + step, piece)
                pass_message(step, piece).start()

    lower_lanes = lax.broadcasted_iota(jnp.int32, (count, 2 * count), 1) < count

    def assemble(row):
        @pl.loop(0, ORB)
        def _(i):
            for j in range(ORB):
                here = tiles[row + 1, i * ORB + j]
                right_mat[row, place(i), j * 128 : (j + 1) * 128] = here.astype(BF16)
                both = jnp.concatenate([tiles[row, i * ORB + j], here], 0).T
                left_mat[
                    row, j * count : (j + 1) * count, pl.ds(pl.multiple_of(i * 128, 128), 128)
                ] = jnp.where(lower_lanes, both[count:], both[:count]).astype(BF16)

    network(0)
    hand_on(0)
    network(1)
    hand_on(1)
    assemble(0)
    network(2)
    hand_on(2)
    assemble(1)
    hand_on(3)

    def onsite_of(k):
        kind = poss[base + k][3:4, 0:count]
        pick = (lax.broadcasted_iota(jnp.int32, (SPECIES, count), 0).astype(F32) == kind).astype(F32)
        return lax.dot_general(
            pick,
            onsite_table[...],
            (((0,), (0,)), ((), ())),
            precision=lax.Precision.HIGHEST,
            preferred_element_type=F32,
        )

    def apply(vec, row, onsite, at):
        span = slice(at * COLS_STEP, (at + 1) * COLS_STEP)
        start = row * count
        if not isinstance(row, int):
            start = pl.multiple_of(start, count)
        after = vec[:, pl.ds(start + count, 2 * count), span]
        before = vec[:, pl.ds(start, 2 * count), span]
        here = after[:, 0:count].astype(F32)
        after = after.reshape(ORB * 2 * count, COLS_STEP)
        before = before.reshape(ORB * 2 * count, COLS_STEP)
        result = dot(right_mat[row], after) + dot(left_mat[row], before)
        return [
            result[i * count : (i + 1) * count] + onsite[:, i : i + 1] * here[i]
            for i in range(ORB)
        ]

    onsites = [onsite_of(1), onsite_of(2)]
    far = 2 * odd
    y_copies = []
    steps = cols // COLS_STEP
    for at in range(steps):
        span = slice(at * COLS_STEP, (at + 1) * COLS_STEP)
        for piece in range(at * COLS_STEP // SEND_STEP, (at + 1) * COLS_STEP // SEND_STEP):
            arrived(3 - 3 * odd, piece)

            @pl.when(jnp.logical_not(middle))
            def _():
                for step in range(2):
                    arrived(far + step, piece)

        for row in range(2):
            step = apply(xx, row, onsites[row], at)
            for i in range(ORB):
                yy[i, (row + 1) * count : (row + 2) * count, span] = step[i].astype(BF16)
        y_copies.append(
            message(
                yy.at[:, place(own), span],
                yy.at[:, place(peer_place), span],
                y_send.at[at],
                y_recv.at[at],
                peer,
            )
        )
        y_copies[at].start()
    for k in range(lane_blocks):
        lanes = slice(k * 128, (k + 1) * 128)
        for i in range(ORB):
            rows[k, pl.ds(i, count, stride=ORB), :] = yy[i, place(own), lanes].astype(F32)
        first_out[:, lanes] = rows[k].astype(BF16)

    onsite = jnp.where(odd == 1, onsites[0], onsites[1])
    for at in range(steps):
        span = slice(at * COLS_STEP, (at + 1) * COLS_STEP)
        y_copies[at].wait_recv()
        step = apply(yy, own - 1, onsite, at)
        for i in range(ORB):
            value = 2.0 * step[i] - xx[i, place(own), span].astype(F32)
            for k in range(COLS_STEP // 128):
                rows[at * (COLS_STEP // 128) + k, pl.ds(i, count, stride=ORB), :] = value[
                    :, k * 128 : (k + 1) * 128
                ]
        for k in range(COLS_STEP // 128):
            block = at * (COLS_STEP // 128) + k
            filtered_out[:, block * 128 : (block + 1) * 128] = rows[block]

    for copy in small + y_copies:
        copy.wait_send()
    for piece in range(pieces):
        cross_message(piece).wait_send()
        peer_message(piece).wait_send()

        @pl.when(middle)
        def _():
            for step in range(2):
                pass_message(step, piece).wait_send()


def on_device(
    node_feat,
    species,
    positions,
    pair_second,
    pair_mask,
    x_vec,
    species_table,
    onsite_table,
    w_first,
    w_second,
    w_radial,
    w_out,
):
    count = node_feat.shape[0]
    orbs, cols = x_vec.shape
    slots = pair_second.shape[0]
    steps, pieces = cols // COLS_STEP, cols // SEND_STEP
    vmem = pl.BlockSpec(memory_space=pltpu.VMEM)
    return pl.pallas_call(
        kernel,
        out_shape=(
            jax.ShapeDtypeStruct((orbs, cols), BF16),
            jax.ShapeDtypeStruct((orbs, cols), F32),
        ),
        in_specs=[vmem] * 12,
        out_specs=(vmem, vmem),
        scratch_shapes=[
            pltpu.VMEM((5, count, node_feat.shape[1]), BF16),
            pltpu.VMEM((5, 8, 128), F32),
            pltpu.VMEM((5, 1, slots), jnp.int32),
            pltpu.VMEM((cols // 128, orbs, 128), F32),
            pltpu.VMEM((ORB, 4 * count, cols), BF16),
            pltpu.VMEM((ORB, 4 * count, cols), BF16),
            pltpu.VMEM((3, ORB * ORB, count, 128), F32),
            pltpu.VMEM((2, orbs, ORB * 128), BF16),
            pltpu.VMEM((2, orbs, ORB * 128), BF16),
            pltpu.SemaphoreType.DMA((12,)),
            pltpu.SemaphoreType.DMA((12,)),
            pltpu.SemaphoreType.DMA((pieces,)),
            pltpu.SemaphoreType.DMA((pieces,)),
            pltpu.SemaphoreType.DMA((2, pieces)),
            pltpu.SemaphoreType.DMA((4, pieces)),
            pltpu.SemaphoreType.DMA((steps,)),
            pltpu.SemaphoreType.DMA((steps,)),
        ],
        compiler_params=pltpu.CompilerParams(
            collective_id=0, has_side_effects=True, vmem_limit_bytes=58 * 2**20
        ),
        name="pair_filter",
    )(
        node_feat,
        species.reshape(1, count),
        positions.T,
        pair_second.reshape(1, slots),
        pair_mask.reshape(1, slots),
        x_vec,
        species_table,
        onsite_table,
        w_first,
        w_second,
        w_radial,
        w_out.T,
    )


def solution(mesh):
    split = P(("groups", "atoms"))
    rows = P(("groups", "atoms"), None)
    return jax.shard_map(
        on_device,
        mesh=mesh,
        in_specs=(rows, split, rows, split, split, rows) + (P(),) * 6,
        out_specs=(rows, rows),
        check_vma=False,
    )
```

```python
import functools

import jax
import jax.numpy as jnp
from jax import lax
from jax.experimental import pallas as pl
from jax.experimental.pallas import tpu as pltpu
from jax.sharding import PartitionSpec as P

ORB = 13
NRBF = 32
SPECIES = 2
NEIGH = 32
MESH = pl.DeviceIdType.MESH
F32, BF16 = jnp.float32, jnp.bfloat16
CHUNK = 512
GROUP = 8
COLS_STEP = 256
SEND_STEP = 128


def dot(a, b):
    return jnp.dot(a, b, preferred_element_type=F32)


def dot_tn(a, b):
    return lax.dot_general(a, b, (((0,), (0,)), ((), ())), preferred_element_type=F32)


def dot_nt(a, b):
    return lax.dot_general(a, b, (((1,), (1,)), ((), ())), preferred_element_type=F32)


def split_two(v):
    high = v.astype(BF16)
    return [high, (v - high.astype(F32)).astype(BF16)]


def split_three(v):
    high = v.astype(BF16).astype(F32)
    rest = v - high
    middle = rest.astype(BF16).astype(F32)
    return jnp.concatenate([high, middle, rest - middle, jnp.zeros_like(v)], 0).astype(BF16)


def pair_tiles(own_code_at, pos_first, pos_window, terms, w_out, scale, width, tiles):
    count = tiles.shape[1]
    per_chunk = CHUNK // NEIGH
    lanes = lax.broadcasted_iota(jnp.int32, (1, CHUNK), 1) // NEIGH
    atom = lax.broadcasted_iota(jnp.int32, (count, CHUNK), 0)
    second = lax.broadcasted_iota(jnp.int32, (128, CHUNK), 0)
    centres = lax.broadcasted_iota(jnp.int32, (NRBF, 1), 0).astype(F32) * (2.0 / (NRBF - 1))
    diagonal = (
        lax.broadcasted_iota(jnp.int32, (GROUP, GROUP * NEIGH), 1) // NEIGH
        == lax.broadcasted_iota(jnp.int32, (GROUP, GROUP * NEIGH), 0)
    ).astype(F32)
    pairs = tiles.shape[0]

    @pl.loop(0, count // per_chunk)
    def _(at):
        code = own_code_at(at)
        pick_first = (atom == lanes + at * per_chunk).astype(F32).astype(BF16)
        pick_all = (second == code).astype(F32).astype(BF16)
        pick_second = pick_all[:width]
        parts = dot(pos_first, pick_first) - dot(pos_window, pick_second)
        diff = (parts[0:8] + parts[8:16] + parts[16:24])[0:3]
        dist_sq = jnp.sum(diff * diff, axis=0, keepdims=True)
        radial = jnp.exp(-(((dist_sq / 64.0 - centres) * 8.0) ** 2)).astype(BF16)
        picks = jnp.concatenate([pick_first, pick_first, pick_second, pick_second, radial], 0)
        pre = dot(terms, picks)
        half = pre * 0.5
        hidden = (half + half * jnp.tanh(half)).astype(BF16)
        blocks = dot(w_out, hidden) * scale
        for group in range(per_chunk // GROUP):
            span = slice(group * GROUP * NEIGH, (group + 1) * GROUP * NEIGH)
            spread = (blocks[:, None, span] * diagonal[None]).reshape(pairs * GROUP, GROUP * NEIGH)
            placed = dot_nt(spread.astype(BF16), pick_all[:, span])
            start = pl.multiple_of((at * (per_chunk // GROUP) + group) * GROUP, GROUP)
            tiles[:, pl.ds(start, GROUP), :] = placed.reshape(pairs, GROUP, 128)


def kernel(
    node_feat,
    species,
    positions,
    pair_second,
    pair_mask,
    x_vec,
    species_table,
    onsite_table,
    w_first,
    w_second,
    w_radial,
    w_out,
    first_out,
    filtered_out,
    feats,
    poss,
    codes,
    rows,
    xx,
    yy,
    tiles,
    right_mat,
    left_mat,
    small_send,
    small_recv,
    peer_send,
    cross_send,
    pass_send,
    x_recv,
    y_send,
    y_recv,
):
    n = lax.axis_size("atoms")
    me = lax.axis_index("atoms")
    spot = lax.rem(me, 4)
    odd = lax.rem(me, 2)
    own = 2 - odd
    peer = me + 1 - 2 * odd
    peer_place = 3 * odd
    upper_half = spot // 2
    cross_to = me - spot + 2 - upper_half
    middle = (spot == 1) | (spot == 2)
    pass_to = lax.rem(jnp.where(spot == 1, me + 3, me + n - 3), n)
    pass_from = 2 - 2 * upper_half
    pass_place = 2 * upper_half
    count = node_feat.shape[0]
    cols = x_vec.shape[1]
    lane_blocks = cols // 128
    pieces = cols // SEND_STEP

    def at_distance(d):
        return lax.rem(me + n + d, n)

    near = (-2, -1, 1, 2)
    barrier = pltpu.get_barrier_semaphore()
    for d in (-3, -2, -1, 1, 2, 3):
        pl.semaphore_signal(barrier, inc=1, device_id={"atoms": at_distance(d)}, device_id_type=MESH)

    def message(src, dst, send_sem, recv_sem, to):
        return pltpu.make_async_remote_copy(
            src_ref=src,
            dst_ref=dst,
            send_sem=send_sem,
            recv_sem=recv_sem,
            device_id={"atoms": to},
            device_id_type=MESH,
        )

    spec = species[...]
    onehot = (lax.broadcasted_iota(jnp.int32, (SPECIES, count), 0) == spec).astype(F32)
    feats[2] = (
        node_feat[...].astype(F32) + dot_tn(onehot.astype(BF16), species_table[...])
    ).astype(BF16)
    poss[2] = jnp.zeros(poss.shape[1:], F32)
    poss[2, 0:3, 0:count] = positions[...]
    poss[2, 3:4, 0:count] = spec.astype(F32)
    codes[2] = jnp.where(pair_mask[...] != 0, pair_second[...], 255)

    def place(where):
        return pl.ds(pl.multiple_of(where * count, count), count)

    for k in range(lane_blocks):
        rows[k] = x_vec[:, k * 128 : (k + 1) * 128].astype(F32)
        for i in range(ORB):
            xx[i, place(own), k * 128 : (k + 1) * 128] = rows[
                k, pl.ds(i, count, stride=ORB), :
            ].astype(BF16)
    pl.semaphore_wait(barrier, 6)

    small = []
    for which, d in enumerate(near):
        for kind, array in enumerate((feats, poss, codes)):
            small.append(
                message(
                    array.at[2],
                    array.at[2 - d],
                    small_send.at[3 * which + kind],
                    small_recv.at[3 * which + kind],
                    at_distance(d),
                )
            )
    for copy in small:
        copy.start()

    def x_message(from_place, to_place, piece, send_sem, to):
        span = slice(piece * SEND_STEP, (piece + 1) * SEND_STEP)
        return message(
            xx.at[:, place(from_place), span],
            xx.at[:, place(to_place), span],
            send_sem,
            x_recv.at[to_place, piece],
            to,
        )

    def cross_message(piece):
        return x_message(own, spot, piece, cross_send.at[piece], cross_to)

    def peer_message(piece):
        return x_message(own, peer_place, piece, peer_send.at[piece], peer)

    def pass_message(step, piece):
        return x_message(
            pass_from + step, pass_place + step, piece, pass_send.at[step, piece], pass_to
        )

    def arrived(where, piece):
        span = slice(piece * SEND_STEP, (piece + 1) * SEND_STEP)
        there = xx.at[:, place(where), span]
        message(there, there, peer_send.at[piece], x_recv.at[where, piece], peer).wait_recv()

    for piece in range(pieces):
        cross_message(piece).start()
    for piece in range(pieces):
        peer_message(piece).start()

    scale = 1.0 / jnp.sqrt(jnp.float32(2 * ORB * NEIGH))
    base = 2 - own
    for copy in small:
        copy.wait_recv()

    seconds = [dot(feats[base + k], w_second[...]) for k in range(4)]
    sites = [split_three(poss[base + k][:, 0:count]) for k in range(4)]

    def network(k):
        window = jnp.concatenate([seconds[k], seconds[k + 1]], 0)
        terms = jnp.concatenate(
            split_two(dot(feats[base + k], w_first[...])) + split_two(window) + [w_radial[...]], 0
        )

        def code(at):
            return codes[base + k, :, pl.ds(pl.multiple_of(at * CHUNK, CHUNK), CHUNK)]

        pair_tiles(
            code, sites[k], jnp.concatenate([sites[k], sites[k + 1]], 1),
            terms.astype(F32).T.astype(BF16), w_out[...], scale, 2 * count, tiles.at[k],
        )

    def hand_on(piece):
        @pl.when(middle)
        def _():
            for step in range(2):
                arrived(pass_from + step, piece)
                pass_message(step, piece).start()

    lower_lanes = lax.broadcasted_iota(jnp.int32, (count, 2 * count), 1) < count

    def assemble(row):
        @pl.loop(0, ORB)
        def _(i):
            for j in range(ORB):
                here = tiles[row + 1, i * ORB + j]
                right_mat[row, place(i), j * 128 : (j + 1) * 128] = here.astype(BF16)
                both = jnp.concatenate([tiles[row, i * ORB + j], here], 0).T
                left_mat[
                    row, j * count : (j + 1) * count, pl.ds(pl.multiple_of(i * 128, 128), 128)
                ] = jnp.where(lower_lanes, both[count:], both[:count]).astype(BF16)

    network(0)
    hand_on(0)
    network(1)
    hand_on(1)
    assemble(0)
    network(2)
    hand_on(2)
    assemble(1)
    hand_on(3)

    def onsite_of(k):
        kind = poss[base + k][3:4, 0:count]
        pick = (lax.broadcasted_iota(jnp.int32, (SPECIES, count), 0).astype(F32) == kind).astype(F32)
        return lax.dot_general(
            pick,
            onsite_table[...],
            (((0,), (0,)), ((), ())),
            precision=lax.Precision.HIGHEST,
            preferred_element_type=F32,
        )

    def apply(vec, row, onsite, at):
        span = slice(at * COLS_STEP, (at + 1) * COLS_STEP)
        start = row * count
        if not isinstance(row, int):
            start = pl.multiple_of(start, count)
        after = vec[:, pl.ds(start + count, 2 * count), span]
        before = vec[:, pl.ds(start, 2 * count), span]
        here = after[:, 0:count].astype(F32)
        after = after.reshape(ORB * 2 * count, COLS_STEP)
        before = before.reshape(ORB * 2 * count, COLS_STEP)
        result = dot(right_mat[row], after) + dot(left_mat[row], before)
        return [
            result[i * count : (i + 1) * count] + onsite[:, i : i + 1] * here[i]
            for i in range(ORB)
        ]

    onsites = [onsite_of(1), onsite_of(2)]
    far = 2 * odd
    y_copies = []
    steps = cols // COLS_STEP
    for at in range(steps):
        span = slice(at * COLS_STEP, (at + 1) * COLS_STEP)
        for piece in range(at * COLS_STEP // SEND_STEP, (at + 1) * COLS_STEP // SEND_STEP):
            arrived(3 - 3 * odd, piece)

            @pl.when(jnp.logical_not(middle))
            def _():
                for step in range(2):
                    arrived(far + step, piece)

        for row in range(2):
            step = apply(xx, row, onsites[row], at)
            for i in range(ORB):
                yy[i, (row + 1) * count : (row + 2) * count, span] = step[i].astype(BF16)
        y_copies.append(
            message(
                yy.at[:, place(own), span],
                yy.at[:, place(peer_place), span],
                y_send.at[at],
                y_recv.at[at],
                peer,
            )
        )
        y_copies[at].start()
    for k in range(lane_blocks):
        lanes = slice(k * 128, (k + 1) * 128)
        for i in range(ORB):
            rows[k, pl.ds(i, count, stride=ORB), :] = yy[i, place(own), lanes].astype(F32)
        first_out[:, lanes] = rows[k].astype(BF16)

    onsite = jnp.where(odd == 1, onsites[0], onsites[1])
    for at in range(steps):
        span = slice(at * COLS_STEP, (at + 1) * COLS_STEP)
        y_copies[at].wait_recv()
        step = apply(yy, own - 1, onsite, at)
        for i in range(ORB):
            value = 2.0 * step[i] - xx[i, place(own), span].astype(F32)
            for k in range(COLS_STEP // 128):
                rows[at * (COLS_STEP // 128) + k, pl.ds(i, count, stride=ORB), :] = value[
                    :, k * 128 : (k + 1) * 128
                ]
        for k in range(COLS_STEP // 128):
            block = at * (COLS_STEP // 128) + k
            filtered_out[:, block * 128 : (block + 1) * 128] = rows[block]

    for copy in small + y_copies:
        copy.wait_send()
    for piece in range(pieces):
        cross_message(piece).wait_send()
        peer_message(piece).wait_send()

        @pl.when(middle)
        def _():
            for step in range(2):
                pass_message(step, piece).wait_send()


def on_device(
    node_feat,
    species,
    positions,
    pair_second,
    pair_mask,
    x_vec,
    species_table,
    onsite_table,
    w_first,
    w_second,
    w_radial,
    w_out,
):
    count = node_feat.shape[0]
    orbs, cols = x_vec.shape
    slots = pair_second.shape[0]
    steps, pieces = cols // COLS_STEP, cols // SEND_STEP
    vmem = pl.BlockSpec(memory_space=pltpu.VMEM)
    return pl.pallas_call(
        kernel,
        out_shape=(
            pltpu.VMEM((orbs, cols), BF16),
            pltpu.VMEM((orbs, cols), F32),
        ),
        in_specs=[vmem] * 12,
        out_specs=(vmem, vmem),
        scratch_shapes=[
            pltpu.VMEM((5, count, node_feat.shape[1]), BF16),
            pltpu.VMEM((5, 8, 128), F32),
            pltpu.VMEM((5, 1, slots), jnp.int32),
            pltpu.VMEM((cols // 128, orbs, 128), F32),
            pltpu.VMEM((ORB, 4 * count, cols), BF16),
            pltpu.VMEM((ORB, 4 * count, cols), BF16),
            pltpu.VMEM((3, ORB * ORB, count, 128), F32),
            pltpu.VMEM((2, orbs, ORB * 128), BF16),
            pltpu.VMEM((2, orbs, ORB * 128), BF16),
            pltpu.SemaphoreType.DMA((12,)),
            pltpu.SemaphoreType.DMA((12,)),
            pltpu.SemaphoreType.DMA((pieces,)),
            pltpu.SemaphoreType.DMA((pieces,)),
            pltpu.SemaphoreType.DMA((2, pieces)),
            pltpu.SemaphoreType.DMA((4, pieces)),
            pltpu.SemaphoreType.DMA((steps,)),
            pltpu.SemaphoreType.DMA((steps,)),
        ],
        compiler_params=pltpu.CompilerParams(
            collective_id=0, has_side_effects=True, vmem_limit_bytes=58 * 2**20
        ),
        name="pair_filter",
    )(
        node_feat,
        species.reshape(1, count),
        positions.T,
        pair_second.reshape(1, slots),
        pair_mask.reshape(1, slots),
        x_vec,
        species_table,
        onsite_table,
        w_first,
        w_second,
        w_radial,
        w_out.T,
    )


def solution(mesh):
    split = P(("groups", "atoms"))
    rows = P(("groups", "atoms"), None)
    return jax.shard_map(
        on_device,
        mesh=mesh,
        in_specs=(rows, split, rows, split, split, rows) + (P(),) * 6,
        out_specs=(rows, rows),
        check_vma=False,
    )
```
